128 devices in a mesh: mode: 8 (over y_hi, x), space: 16 (over z, y_lo, core).
Axes of the slice: x: 4, y: 4 (y_hi: 2, y_lo: 2; y = y_hi * 2 + y_lo), z: 4, core: 2. Of those that a mesh axis runs over, the one named last changes fastest.
Arguments:
- resident: bfloat16 [2, 8192, 8, 4096], P(None, 'mode', None, 'space'), may hold values from -0.0625 to 0.0625
- source: bfloat16 [2, 768, 8, 4096], P(None, 'mode', None, 'space'), may hold values from -6 to 6
- insertion: bfloat16 [4, 768, 1024], replicated, may hold values from -0.21875 to 0.21875
- owners: int32 [256, 1], P('mode'), may hold values from 0 to 15; in each aligned block of 32 rows (0 to 31, 32 to 63, ...) at most 4 rows name the same one
- diag_time: int32 [4], replicated, may hold values from 0 to 7
- diag_mom: int32 [4], replicated, may hold values from 1 to 4
Outputs:
- mesons: bfloat16 [64, 2, 1024, 1024], P('space', None, 'mode')
The draws below stay inside these ranges and needn't reach their ends.
Inputs may be any that keep to these rules, and one draw needn't show every extreme that they name: `owners`: within the 32 strips of one index of mode, no owner is named more than 4 times.
All inputs are finite; a program needn't handle non-finite values.
Results may differ from the reference program's by a relative error of at most 0.019.
Values may be sent and summed in bfloat16 or wider, within the bound.
No kernel may reach another device: no remote copies, remote signals or barrier semaphores. Data moves between devices by JAX's collectives and lax.ppermute only.
A program may use at most 192 MiB of HBM per device.

```python
import math
import jax
import jax.numpy as jnp
import numpy as np
from jax import lax

SRC = 768
RES_DEV = 1024
RES = 8192
STRIP = 128
OUTW = 1024
SLAB = 256
SPACE_SITES = 4096
NT = 8
DIAG = 4
NMOM = 4
LX = 96
CAP = 4
STRIPS_DEV = 32
N_MODE = 8
N_SPACE = 16


def touch_ends(entries, stream_key, low, top_value):
    place = [jax.random.randint(jax.random.fold_in(stream_key, axis), (), 0, length) for axis, length in enumerate(entries.shape)]
    longest = entries.shape.index(max(entries.shape))
    beside = place[:longest] + [(place[longest] + 1) % entries.shape[longest]] + place[longest + 1:]
    return entries.at[tuple(place)].set(low).at[tuple(beside)].set(top_value)


def levels(key, extent, pieces, least, high):
    def one(position, blocks):
        draws = jax.random.uniform(jax.random.fold_in(jax.random.fold_in(key, 6), position), (blocks,), jnp.float32, least / len(pieces), high / len(pieces))
        return jnp.repeat(jnp.exp(draws), extent[position] // blocks).reshape((-1,) + (1,) * (len(extent) - position - 1))

    loudness = one(*pieces[0])
    for cut in pieces[1:]:
        loudness = loudness * one(*cut)
    return loudness


def assign_block(key, own, number, rows, number_of, top, bound, lean):
    order = jax.random.permutation(key, number_of)
    heavy_load, common = portions_of(number_of, rows * top, bound, lean, True), portions_of(number_of, rows * top, bound, lean, False)
    places = jnp.arange(number_of)

    def named(lengths, turn):
        used = int((lengths > 0).sum())
        fixed = max(1, used // 4)
        shifted = fixed + (places - fixed + turn * (used - fixed)) % max(1, number_of - fixed)
        return jnp.zeros((number_of,), jnp.int32).at[order[jnp.where(places < fixed, places, shifted)]].set(jnp.asarray(lengths, jnp.int32))

    lengths = jnp.where(number % 4 == 0, named(heavy_load, number // 4), named(common, number - number // 4 - 1))
    mixed = jax.random.permutation(jax.random.fold_in(own, 3), number_of)
    giver, sink = mixed[0:number_of // 2 * 2:2], mixed[1:number_of // 2 * 2:2]
    room = jnp.minimum(lengths[giver] - 1, bound - lengths[sink]) // 2
    room = jnp.where((giver == order[0]) | (sink == order[0]) | (lengths[sink] == 0), 0, jnp.maximum(room, 0))
    shifted = jax.random.randint(jax.random.fold_in(own, 4), (number_of // 2,), 0, 1 << 20) % (room + 1)
    lengths = lengths.at[giver].add(-shifted).at[sink].add(shifted)
    labels = jnp.searchsorted(jnp.cumsum(lengths), jnp.arange(rows * top), side="right").astype(jnp.int32)
    table = labels.reshape(top, rows).T
    table = table[jax.random.permutation(jax.random.fold_in(own, 1), rows)]
    turn = jax.random.randint(jax.random.fold_in(own, 2), (rows, 1), 0, top)
    return jnp.take_along_axis(table, (jnp.arange(top)[None, :] + turn) % top, axis=1)


def portions_of(number_of, total, reach, slope, full):
    loads = [(1 << 20) // math.isqrt(rank ** slope) + 1 for rank in range(1, number_of + 1)]
    largest = reach if full else min(reach, max(-(-total // number_of), total * loads[0] // sum(loads)))
    least = 1 if total - largest >= number_of - 1 else 0
    given, surplus = [largest] + [least] * (number_of - 1), total - largest - least * (number_of - 1)
    while surplus > 0:
        candidates = [i for i in range(1, number_of) if given[i] < largest] or [i for i in range(1, number_of) if given[i] < reach]
        pool, remaining = sum([loads[i] for i in candidates]), surplus
        for i in candidates:
            extra = min(reach - given[i], max(1, remaining * loads[i] // pool), surplus)
            given[i] = given[i] + extra
            surplus = surplus - extra
    return np.array(given)


def noise(own_key, dims, width, most, pieces=(), held_as=jnp.bfloat16):
    entries = jax.random.normal(own_key, dims, jnp.float32) * width
    if len(pieces) > 0:
        entries = levels(own_key, dims, pieces, -0.22, 0.18) * entries
    return jnp.clip(entries, min=-most, max=most).astype(held_as)


def setup_inputs(seed: int = 0) -> dict:
    seeds = jax.random.split(jax.random.key(seed), 7)
    resident = noise(seeds[0], (2, RES, NT, SPACE_SITES), (2 * SLAB * N_SPACE) ** -0.5, 0.0625, ((1, 8), (3, 16)))
    source = noise(seeds[1], (2, SRC, NT, SPACE_SITES), 1.0, 6.0, ((1, 8), (3, 16)))
    insertion = noise(seeds[2], (DIAG, SRC, OUTW), SRC ** -0.5, 0.21875)
    owners_keys = jax.random.split(jax.random.fold_in(seeds[3], 1), (N_MODE * STRIPS_DEV) // STRIPS_DEV)
    owners_turns = jax.random.permutation(jax.random.fold_in(seeds[3], 3), (N_MODE * STRIPS_DEV) // STRIPS_DEV)
    owners = jax.vmap(lambda own, number: assign_block(jax.random.fold_in(seeds[3], 2), own, number, STRIPS_DEV, N_SPACE, 1, CAP, 2))(owners_keys, owners_turns).reshape((N_MODE * STRIPS_DEV, 1))
    diag_time = touch_ends(jax.random.randint(seeds[4], (DIAG,), 0, NT), jax.random.fold_in(seeds[4], 1), 0, NT - 1).astype(jnp.int32)
    diag_mom = touch_ends(jax.random.randint(seeds[5], (DIAG,), 1, NMOM + 1), jax.random.fold_in(seeds[5], 1), 1, NMOM).astype(jnp.int32)
    return {"resident": resident, "source": source, "insertion": insertion, "owners": owners, "diag_time": diag_time, "diag_mom": diag_mom}


def phase_pair(momentum, start, count):
    lattice_positions = (start + jnp.arange(count, dtype=jnp.int32)) % LX
    turns = (momentum * lattice_positions) % LX
    angle = (2.0 * math.pi / LX) * turns.astype(jnp.float32)
    return jnp.cos(angle), jnp.sin(angle)


def one_field(res_slice, src_slice, momentum):
    def accumulate_portion(total, shard):
        start = (shard * SLAB).astype(jnp.int32)
        res_part = lax.dynamic_slice_in_dim(res_slice, start, SLAB, 2).astype(jnp.float32)
        src_part = lax.dynamic_slice_in_dim(src_slice, start, SLAB, 2)
        cosine, sine = phase_pair(momentum, start, SLAB)
        real_in = res_part[0] * cosine[None, :] - res_part[1] * sine[None, :]
        imag_in = -(res_part[0] * sine[None, :] + res_part[1] * cosine[None, :])
        phased = jnp.stack([real_in, imag_in]).astype(jnp.bfloat16)
        combos = jnp.einsum("prx,qsx->pqrs", phased.astype(jnp.float32), src_part.astype(jnp.float32))
        real_out = combos[0, 0] - combos[1, 1]
        imag_out = combos[0, 1] + combos[1, 0]
        term = jnp.stack([real_out, imag_out]).astype(jnp.bfloat16)
        term = lax.optimization_barrier(term)
        return total + term.astype(jnp.float32), None

    total, unused = lax.scan(accumulate_portion, jnp.zeros((2, RES, SRC), jnp.float32), jnp.arange(N_SPACE, dtype=jnp.int32))
    return total.astype(jnp.bfloat16)


def reference(resident, source, insertion, owners, diag_time, diag_mom):
    fields = []
    for diagram in range(DIAG):
        res_slice = jnp.take(resident, diag_time[diagram], axis=2)
        src_slice = jnp.take(source, diag_time[diagram], axis=2)
        fields.append(one_field(res_slice, src_slice, diag_mom[diagram]))
    field = jnp.stack(fields)
    blocks = RES_DEV // STRIP
    band_list = field.reshape(DIAG, 2, N_MODE, blocks, STRIP, SRC).transpose(2, 0, 3, 1, 4, 5)
    band_list = band_list.reshape(N_MODE, STRIPS_DEV, 2, STRIP, SRC)
    strip_diag = jnp.arange(STRIPS_DEV, dtype=jnp.int32) // blocks
    selected_targets = jnp.take(insertion, strip_diag, axis=0)
    product = jnp.einsum("mkpas,kso->mkpao", band_list.astype(jnp.float32), selected_targets.astype(jnp.float32)).astype(jnp.bfloat16)
    owner_list = owners[:, 0].reshape(N_MODE, STRIPS_DEV)
    same = owner_list[:, :, None] == owner_list[:, None, :]
    order = jnp.arange(STRIPS_DEV, dtype=jnp.int32)
    earlier = order[None, :] < order[:, None]
    rank = jnp.sum((same & earlier[None, :, :]).astype(jnp.int32), axis=2)
    slot = owner_list * CAP + rank
    mode_grid = jnp.broadcast_to(jnp.arange(N_MODE, dtype=jnp.int32)[:, None], (N_MODE, STRIPS_DEV))
    mesons = jnp.zeros((N_SPACE * CAP, N_MODE, 2, STRIP, OUTW), jnp.bfloat16)
    mesons = mesons.at[slot, mode_grid].set(product)
    return mesons.transpose(0, 2, 1, 3, 4).reshape(N_SPACE * CAP, 2, N_MODE * STRIP, OUTW)
```

```python
import functools
import math

import jax
import jax.numpy as jnp
from jax import lax
from jax.experimental import pallas as pl
from jax.experimental.pallas import tpu as pltpu
from jax.sharding import PartitionSpec as P

STRIP = 128
LX = 96
CAP = 4
BF = jnp.bfloat16
F32 = jnp.float32
VMEM_LIMIT = 48 * 1024 * 1024


def phase_pair(diag_mom, start, count):
    lattice_positions = (start + jnp.arange(count, dtype=jnp.int32)) % LX
    turns = diag_mom[:, None] * lattice_positions[None, :] % LX
    angle = 2.0 * math.pi / LX * turns.astype(F32)
    return jnp.cos(angle), jnp.sin(angle)


def params():
    return pltpu.CompilerParams(vmem_limit_bytes=VMEM_LIMIT)


def cost(flops, size):
    return pl.CostEstimate(flops=flops, bytes_accessed=size, transcendentals=0)


LANES = 128


def widen(ref, wide):
    parts, rows, times, _ = ref.shape
    for p in range(parts):
        for h in range(wide.shape[1]):
            x = ref[p, :, :, h * LANES : (h + 1) * LANES]
            wide[p, h] = x.astype(F32).reshape(rows * times, LANES)


def narrow(wide, p, rows):
    return jnp.concatenate([wide[p, h, rows, :] for h in range(wide.shape[1])], axis=1)


def source_kernel(meta, cos_ref, sin_ref, src_ref, keep_ref, send_ref, wide):
    parts, modes, times, sites = src_ref.shape
    half = modes // 2
    widen(src_ref, wide)
    core = meta[5]
    for d in range(keep_ref.shape[0]):
        c = cos_ref[d : d + 1, :]
        s = sin_ref[d : d + 1, :]
        for ref, who in ((keep_ref, core), (send_ref, 1 - core)):
            rows = pl.ds(who * (half * times) + meta[d], half, stride=times)
            re = narrow(wide, 0, rows)
            im = narrow(wide, 1, rows)
            ref[d, :, 0:sites] = (re * c + im * s).astype(BF)
            ref[d, :, sites : 2 * sites] = (im * c - re * s).astype(BF)


def source_slices(meta, cosine, sine, source):
    parts, modes, times, sites = source.shape
    diagrams = cosine.shape[0]
    piece = jax.ShapeDtypeStruct((diagrams, modes // 2, parts * sites), BF)
    return pl.pallas_call(
        source_kernel,
        out_shape=(piece, piece),
        in_specs=[pl.BlockSpec(memory_space=pltpu.SMEM)]
        + [pl.BlockSpec(memory_space=pltpu.VMEM)] * 3,
        out_specs=[pl.BlockSpec(memory_space=pltpu.VMEM)] * 2,
        scratch_shapes=[pltpu.VMEM((parts, sites // LANES, modes * times, LANES), F32)],
        compiler_params=params(),
        cost_estimate=cost(10**6, 2 * 10**6),
        name="source_slices",
    )(meta, cosine, sine, source)


def resident_kernel(meta, res_ref, out_ref, wide):
    parts, strip, times, sites = res_ref.shape
    diagrams, groups, _, rows, _ = out_ref.shape
    widen(res_ref, wide)
    for d in range(diagrams):
        for p in range(parts):
            x = narrow(wide, p, pl.ds(meta[d], strip, stride=times)).astype(BF)
            for g in range(groups):
                out_ref[d, g ^ meta[4], 0, :, p * sites : (p + 1) * sites] = x[
                    g * rows : (g + 1) * rows
                ]


def resident_slices(meta, resident, diagrams, groups):
    parts, res_dev, times, sites = resident.shape
    blocks = res_dev // STRIP
    rows = STRIP // groups
    return pl.pallas_call(
        resident_kernel,
        out_shape=jax.ShapeDtypeStruct(
            (diagrams, groups, blocks, rows, parts * sites), BF
        ),
        grid_spec=pltpu.PrefetchScalarGridSpec(
            num_scalar_prefetch=1,
            grid=(blocks,),
            in_specs=[
                pl.BlockSpec((parts, STRIP, times, sites), lambda b, meta: (0, b, 0, 0))
            ],
            out_specs=pl.BlockSpec(
                (diagrams, groups, 1, rows, parts * sites),
                lambda b, meta: (0, 0, b, 0, 0),
            ),
            scratch_shapes=[pltpu.VMEM((parts, sites // LANES, STRIP * times, LANES), F32)],
        ),
        compiler_params=params(),
        cost_estimate=cost(10**7, 13 * 10**6),
        name="resident_slices",
    )(meta, resident)


def field_kernel(
    meta, own_ref, par_ref, a0, a1, a2, b0, b1, b2,
    a_keep, a_send, b_keep, b_send, real_rhs, imag_rhs,
):
    j = pl.program_id(0)
    me = meta[6]
    pieces = (
        ((a0, (0, 4)), (a1, (1, 5)), (a2, (3, 7, 2, 6))),
        ((b0, (0, 4)), (b1, (3, 7)), (b2, (1, 5, 2, 6))),
    )
    modes, width = a0.shape[1:]
    sites = width // 2

    @pl.when(j == 0)
    def _():
        for side, arrays in enumerate(pieces):
            for ref, places in arrays:
                for n, place in enumerate(places):
                    v = ref[n]
                    at = me ^ place
                    real_rhs[side, at] = v
                    imag_rhs[side, at, :, 0:sites] = v[:, sites:]
                    imag_rhs[side, at, :, sites:] = -v[:, 0:sites]

    rows = own_ref.shape[1] * own_ref.shape[2] * own_ref.shape[3]
    own = own_ref[0].reshape(rows, width)
    par = par_ref[0].reshape(rows, width)

    def product(rhs):
        dims = (((1,), (1,)), ((), ()))
        columns = rhs.shape[1] * rhs.shape[2]
        return (
            lax.dot_general(own, rhs[0].reshape(columns, width), dims, preferred_element_type=F32)
            + lax.dot_general(par, rhs[1].reshape(columns, width), dims, preferred_element_type=F32)
        ).astype(BF)

    real = product(real_rhs)
    imag = product(imag_rhs)
    for step, (ra, na, rb, nb) in enumerate(
        ((a_keep, 0, b_keep, 0), (a_send, 0, b_keep, 1), (a_send, 1, b_send, 1), (a_keep, 1, b_send, 0))
    ):

        @pl.when(j == step)
        def _(ra=ra, na=na, rb=rb, nb=nb):
            ra[na] = real
            rb[nb] = imag


def partial_field(d, meta, own, par, side_a, side_b):
    groups, blocks, rows, width = own.shape[1:]
    pair = groups // 4
    modes = side_a[0].shape[1]
    columns = 8 * modes
    out = jax.ShapeDtypeStruct((2, pair * blocks * rows, columns), BF)
    res_spec = pl.BlockSpec(
        (1, pair, blocks, rows, width), lambda j, meta: (d, j, 0, 0, 0)
    )

    def whole(x):
        return pl.BlockSpec(x.shape, lambda j, meta: (0,) * len(x.shape))

    return pl.pallas_call(
        field_kernel,
        out_shape=(out,) * 4,
        grid_spec=pltpu.PrefetchScalarGridSpec(
            num_scalar_prefetch=1,
            grid=(4,),
            in_specs=[res_spec, res_spec] + [whole(x) for x in (*side_a, *side_b)],
            out_specs=[whole(out)] * 4,
            scratch_shapes=[pltpu.VMEM((2, 8, modes, width), BF)] * 2,
        ),
        compiler_params=params(),
        cost_estimate=cost(2 * 1024 * 1024 * 768, 5 * 10**6),
        name=f"field_{d}",
    )(meta, own, par, *side_a, *side_b)


def pack_kernel(diagrams, slot_ref, *refs):
    ins, out_ref, strips = refs[: 3 * diagrams], refs[3 * diagrams], refs[-1]
    blocks = strips.shape[0] // diagrams
    rows, columns = strips.shape[2:]
    for d in range(diagrams):
        own_a, own_b, other = ins[3 * d : 3 * d + 3]
        for p, own in enumerate((own_a, own_b)):
            total = (own[...] + other[p].astype(F32)).astype(BF)
            strips[d * blocks : (d + 1) * blocks, p] = total.reshape(
                blocks, rows, columns
            )

    def one(slot, carry):
        out_ref[slot] = strips[slot_ref[slot]]
        return carry

    lax.fori_loop(0, out_ref.shape[0], one, 0)


def pack(slot_strip, finished, blocks):
    diagrams = len(finished)
    tall, columns = finished[0][0].shape
    rows = tall // blocks
    flat = [x for triple in finished for x in triple]
    return pl.pallas_call(
        functools.partial(pack_kernel, diagrams),
        out_shape=jax.ShapeDtypeStruct((slot_strip.shape[0], 2, rows, columns), BF),
        in_specs=[pl.BlockSpec(memory_space=pltpu.SMEM)]
        + [pl.BlockSpec(memory_space=pltpu.VMEM)] * len(flat),
        out_specs=pl.BlockSpec(memory_space=pltpu.VMEM),
        scratch_shapes=[pltpu.VMEM((diagrams * blocks, 2, rows, columns), BF)],
        compiler_params=params(),
        cost_estimate=cost(10**6, 4 * 10**6),
        name="pack",
    )(slot_strip, *flat)


def insertion_kernel(which, filled, rows_ref, ins_ref, out_ref):
    t = pl.program_id(0)
    columns = rows_ref.shape[-1]
    groups = rows_ref.shape[0] // 2
    width = ins_ref.shape[-1]

    @pl.when(filled[t] == 0)
    def _():
        out_ref[...] = jnp.zeros_like(out_ref)

    @pl.when(filled[t] != 0)
    def _():
        total = None
        for core in range(2):
            lhs = jnp.concatenate(
                [rows_ref[2 * g + core, 0, p] for p in range(2) for g in range(groups)],
                axis=0,
            )
            rhs = ins_ref[0, :, core].reshape(columns, width)
            term = jnp.dot(lhs, rhs, preferred_element_type=F32)
            total = term if total is None else total + term
        out_ref[0] = total.astype(BF).reshape(2, STRIP, width)


def contract(which, filled, received, insertion):
    senders, cap, parts, rows, columns = received.shape
    diagrams, _, width = insertion.shape
    n_mode = 8
    modes = columns // n_mode
    split = insertion.reshape(diagrams, n_mode, 2, modes, width)
    return pl.pallas_call(
        insertion_kernel,
        out_shape=jax.ShapeDtypeStruct((cap, parts, STRIP, width), BF),
        grid_spec=pltpu.PrefetchScalarGridSpec(
            num_scalar_prefetch=2,
            grid=(cap,),
            in_specs=[
                pl.BlockSpec(
                    (senders, 1, parts, rows, columns), lambda t, w, f: (0, t, 0, 0, 0)
                ),
                pl.BlockSpec(
                    (1, n_mode, 2, modes, width), lambda t, w, f: (w[t], 0, 0, 0, 0)
                ),
            ],
            out_specs=pl.BlockSpec(
                (1, parts, STRIP, width), lambda t, w, f: (t, 0, 0, 0)
            ),
        ),
        compiler_params=params(),
        cost_estimate=cost(16 * 10**8, 10**7),
        name="contract",
    )(which, filled, received, split)


def swap(x, axis, bits):
    n = lax.axis_size(axis)
    return lax.ppermute(x, axis, [(i, i ^ bits) for i in range(n)])


Z1, Z3, Y1, CORE = 4, 12, 2, 1
X1, X3, YHI = 1, 3, 4


def slots(owner_list, n_space, me_space):
    strip_count = owner_list.shape[0]
    same = owner_list[:, None] == owner_list[None, :]
    order = jnp.arange(strip_count, dtype=jnp.int32)
    earlier = order[None, :] < order[:, None]
    rank = jnp.sum((same & earlier).astype(jnp.int32), axis=1)
    slot = owner_list * CAP + rank
    numbers = jnp.arange(n_space * CAP, dtype=jnp.int32)
    match = slot[None, :] == numbers[:, None]
    slot_strip = jnp.sum(jnp.where(match, order[None, :], 0), axis=1)
    mine = me_space * CAP + jnp.arange(CAP, dtype=jnp.int32)
    my_match = slot[None, :] == mine[:, None]
    my_strip = jnp.sum(jnp.where(my_match, order[None, :], 0), axis=1)
    filled = jnp.sum(my_match.astype(jnp.int32), axis=1)
    return slot_strip, my_strip, filled


def on_device(resident, source, insertion, owners, diag_time, diag_mom):
    slab = resident.shape[3]
    n_space = lax.axis_size("space")
    diagrams = insertion.shape[0]
    blocks = resident.shape[1] // STRIP
    me_space = lax.axis_index("space")
    me_mode = lax.axis_index("mode")
    meta = jnp.concatenate(
        [diag_time, jnp.stack([me_space // 2, me_space % 2, me_mode]).astype(jnp.int32)]
    )
    cosine, sine = phase_pair(diag_mom, me_space * slab, slab)

    keep, send = source_slices(meta, cosine, sine, source)
    arrived = swap(send, "space", CORE)
    own = resident_slices(meta, resident, diagrams, n_space // 2)
    par = swap(own, "space", CORE)
    slot_strip, my_strip, filled = slots(owners[:, 0], n_space, me_space)

    finished = []
    for d in range(diagrams):
        pair = jnp.stack([keep[d], arrived[d]])
        far = swap(pair, "mode", YHI)
        a0 = jnp.stack([pair[0], far[0]])
        b0 = jnp.stack([pair[1], far[1]])
        a1 = swap(a0, "mode", X1)
        b1 = swap(b0, "mode", X3)
        a2 = swap(jnp.concatenate([a0, a1]), "mode", X3)
        b2 = swap(jnp.concatenate([b0, b1]), "mode", X1)
        a_keep, a_send, b_keep, b_send = partial_field(
            d, meta, own, par, (a0, a1, a2), (b0, b1, b2)
        )
        a_in = swap(a_send, "space", Z1)
        b_in = swap(b_send, "space", Z3)
        a_pass = (a_keep[1].astype(F32) + a_in[1].astype(F32)).astype(BF)
        b_pass = (b_keep[1].astype(F32) + b_in[1].astype(F32)).astype(BF)
        a_last = swap(a_pass, "space", Z3)
        b_last = swap(b_pass, "space", Z1)
        a_sum = a_keep[0].astype(F32) + a_in[0].astype(F32) + a_last.astype(F32)
        b_sum = b_keep[0].astype(F32) + b_in[0].astype(F32) + b_last.astype(F32)
        tall = a_sum.shape[0] // 2
        over_y = swap(jnp.stack([a_sum[tall:], b_sum[tall:]]).astype(BF), "space", Y1)
        finished.append((a_sum[:tall], b_sum[:tall], over_y))

    outgoing = pack(slot_strip, finished, blocks)
    outgoing = outgoing.reshape(n_space, CAP, *outgoing.shape[1:])
    received = lax.all_to_all(outgoing, "space", 0, 0, tiled=True)
    return contract(my_strip // blocks, filled, received, insertion)


def solution(mesh):
    in_specs = (
        P(None, "mode", None, "space"),
        P(None, "mode", None, "space"),
        P(),
        P("mode", None),
        P(),
        P(),
    )
    out_specs = P("space", None, "mode", None)
    return jax.shard_map(
        on_device, mesh=mesh, in_specs=in_specs, out_specs=out_specs, check_vma=False
    )
```

```python
import functools
import math

import jax
import jax.numpy as jnp
from jax import lax
from jax.experimental import pallas as pl
from jax.experimental.pallas import tpu as pltpu
from jax.sharding import PartitionSpec as P

STRIP = 128
LX = 96
CAP = 4
BF = jnp.bfloat16
F32 = jnp.float32
VMEM_LIMIT = 48 * 1024 * 1024


def phase_pair(diag_mom, start, count):
    lattice_positions = (start + jnp.arange(count, dtype=jnp.int32)) % LX
    turns = diag_mom[:, None] * lattice_positions[None, :] % LX
    angle = 2.0 * math.pi / LX * turns.astype(F32)
    return jnp.cos(angle), jnp.sin(angle)


def params():
    return pltpu.CompilerParams(vmem_limit_bytes=VMEM_LIMIT)


def cost(flops, size):
    return pl.CostEstimate(flops=flops, bytes_accessed=size, transcendentals=0)


LANES = 128


def widen(ref, wide):
    parts, rows, times, _ = ref.shape
    for p in range(parts):
        for h in range(wide.shape[1]):
            x = ref[p, :, :, h * LANES : (h + 1) * LANES]
            wide[p, h] = x.astype(F32).reshape(rows * times, LANES)


def narrow(wide, p, rows):
    return jnp.concatenate([wide[p, h, rows, :] for h in range(wide.shape[1])], axis=1)


def source_kernel(ds, meta, cos_ref, sin_ref, src_ref, after_ref, keep_ref, send_ref, wide):
    _, modes, times, sites = src_ref.shape
    half = modes // 2
    widen(src_ref, wide)
    core = meta[5]
    for n, d in enumerate(ds):
        c = cos_ref[d : d + 1, :]
        s = sin_ref[d : d + 1, :]
        for ref, who in ((keep_ref, core), (send_ref, 1 - core)):
            rows = pl.ds(who * (half * times) + meta[d], half, stride=times)
            re = narrow(wide, 0, rows)
            im = narrow(wide, 1, rows)
            ref[n, :, 0:sites] = (re * c + im * s).astype(BF)
            ref[n, :, sites : 2 * sites] = (im * c - re * s).astype(BF)


def source_slices(ds, meta, cosine, sine, source, after):
    parts, modes, times, sites = source.shape
    piece = jax.ShapeDtypeStruct((len(ds), modes // 2, parts * sites), BF)
    return pl.pallas_call(
        functools.partial(source_kernel, ds),
        out_shape=(piece, piece),
        in_specs=[pl.BlockSpec(memory_space=pltpu.SMEM)]
        + [pl.BlockSpec(memory_space=pltpu.VMEM)] * 3
        + [pl.BlockSpec(memory_space=pl.ANY)],
        out_specs=[pl.BlockSpec(memory_space=pltpu.VMEM)] * 2,
        scratch_shapes=[pltpu.VMEM((parts, sites // LANES, modes * times, LANES), F32)],
        compiler_params=params(),
        cost_estimate=cost(10**6, 2 * 10**6),
        name="source_slices",
    )(meta, cosine, sine, source, after)


def resident_kernel(chunks, meta, res_ref, after_ref, *refs):
    outs, wide = refs[:-1], refs[-1]
    parts, strip, times, sites = res_ref.shape
    rows = outs[0].shape[3]
    groups = strip // rows
    z, y = meta[4], meta[7]
    widen(res_ref, wide)
    for out_ref, n, d in [(r, n, d) for r, ds in zip(outs, chunks) for n, d in enumerate(ds)]:
        for p in range(parts):
            x = narrow(wide, p, pl.ds(meta[d], strip, stride=times)).astype(BF)
            for g in range(groups):
                at = ((g % 2) ^ y) * (groups // 2) + ((g // 2) ^ z)
                out_ref[n, at, 0, :, p * sites : (p + 1) * sites] = x[
                    g * rows : (g + 1) * rows
                ]


def resident_slices(chunks, meta, resident, after, groups):
    parts, res_dev, times, sites = resident.shape
    blocks = res_dev // STRIP
    rows = STRIP // groups
    shapes = [(len(ds), groups, blocks, rows, parts * sites) for ds in chunks]
    return pl.pallas_call(
        functools.partial(resident_kernel, chunks),
        out_shape=[jax.ShapeDtypeStruct(shape, BF) for shape in shapes],
        grid_spec=pltpu.PrefetchScalarGridSpec(
            num_scalar_prefetch=1,
            grid=(blocks,),
            in_specs=[
                pl.BlockSpec((parts, STRIP, times, sites), lambda b, meta: (0, b, 0, 0)),
                pl.BlockSpec(memory_space=pl.ANY),
            ],
            out_specs=[
                pl.BlockSpec((*shape[:2], 1, *shape[3:]), lambda b, meta: (0, 0, b, 0, 0))
                for shape in shapes
            ],
            scratch_shapes=[pltpu.VMEM((parts, sites // LANES, STRIP * times, LANES), F32)],
        ),
        compiler_params=params(),
        cost_estimate=cost(30 * 10**9, 13 * 10**6),
        name="resident_slices",
    )(meta, resident, after)


PLACES = (
    ((0, 4), (1, 5), (3, 7, 2, 6)),
    ((0, 4), (3, 7), (1, 5, 2, 6)),
)


def field_kernel(meta, own_ref, par_ref, a0, a1, a2, b0, b1, b2, after_a, after_b,
                 a_keep, a_send, b_keep, b_send, real_rhs, imag_rhs):
    me = meta[6]
    _, groups, blocks, rows, width = own_ref.shape
    sites = width // 2
    columns = real_rhs.shape[1] * real_rhs.shape[2]
    for side, arrays in enumerate(((a0, a1, a2), (b0, b1, b2))):
        for ref, places in zip(arrays, PLACES[side]):
            for n, place in enumerate(places):
                at = me ^ place
                v = ref[n, 0]
                real_rhs[side, at] = v
                imag_rhs[side, at, :, 0:sites] = v[:, sites:]
                imag_rhs[side, at, :, sites:] = -v[:, 0:sites]

    zs = groups // 2
    tall = blocks * rows
    for k in range(2):
        left = [x[0, k * zs : (k + 1) * zs].reshape(zs * tall, width) for x in (own_ref, par_ref)]

        def product(rhs, left=left):
            total = None
            for n, x in enumerate(left):
                term = lax.dot_general(
                    x,
                    rhs[n].reshape(columns, width),
                    (((1,), (1,)), ((), ())),
                    preferred_element_type=F32,
                )
                total = term if total is None else total + term
            return total.astype(BF).reshape(zs, tall, columns)

        real = product(real_rhs)
        imag = product(imag_rhs)
        a_keep[0, 0, k] = real[0]
        a_send[0, 0, k] = real[1]
        a_send[1, 0, k] = real[2]
        a_keep[1, 0, k] = real[3]
        b_keep[0, 0, k] = imag[0]
        b_keep[1, 0, k] = imag[1]
        b_send[1, 0, k] = imag[2]
        b_send[0, 0, k] = imag[3]


def partial_field(n, at, meta, own, par, side_a, side_b, after_a, after_b):
    _, groups, blocks, rows, width = own.shape
    modes = side_a[0].shape[2]
    columns = 8 * modes
    out = jax.ShapeDtypeStruct((2, n, 2, blocks * rows, columns), BF)
    left = pl.BlockSpec(
        (1, groups, blocks, rows, width), lambda i, meta: (at + i, 0, 0, 0, 0)
    )

    def piece(x):
        return pl.BlockSpec((x.shape[0], 1, modes, width), lambda i, meta: (0, i, 0, 0))

    return pl.pallas_call(
        field_kernel,
        out_shape=(out,) * 4,
        grid_spec=pltpu.PrefetchScalarGridSpec(
            num_scalar_prefetch=1,
            grid=(n,),
            in_specs=[left, left]
            + [piece(x) for x in (*side_a, *side_b)]
            + [pl.BlockSpec(memory_space=pl.ANY)] * 2,
            out_specs=[
                pl.BlockSpec((2, 1, *out.shape[2:]), lambda i, meta: (0, i, 0, 0, 0))
            ]
            * 4,
            scratch_shapes=[pltpu.VMEM((2, 8, modes, width), BF)] * 2,
        ),
        compiler_params=params(),
        cost_estimate=cost(n * 2 * 1024 * 1024 * 768, n * 5 * 10**6),
        name="field",
    )(meta, own, par, *side_a, *side_b, after_a, after_b)


def pack_kernel(counts, slot_ref, *refs):
    ins, out_ref, strips = list(refs[:-2]), refs[-2], refs[-1]
    rows, columns = strips.shape[2:]
    at = 0
    for n, size in counts:
        sums = [ins.pop(0) for _ in range(2)]
        other = ins.pop(0) if size == 3 else None
        blocks = sums[0].shape[1] // rows
        for d in range(n):
            for p in range(2):
                total = sums[p][d]
                if other is not None:
                    total = total + other[p, d].astype(F32)
                strips[at : at + blocks, p] = total.astype(BF).reshape(
                    blocks, rows, columns
                )
            at += blocks

    def one(slot, carry):
        out_ref[slot] = strips[slot_ref[slot]]
        return carry

    lax.fori_loop(0, out_ref.shape[0], one, 0)


def pack(slot_strip, finished, strip_count, rows):
    columns = finished[0][0].shape[-1]
    flat = [x for group in finished for x in group]
    counts = [(group[0].shape[0], len(group)) for group in finished]
    return pl.pallas_call(
        functools.partial(pack_kernel, counts),
        out_shape=jax.ShapeDtypeStruct((slot_strip.shape[0], 2, rows, columns), BF),
        in_specs=[pl.BlockSpec(memory_space=pltpu.SMEM)]
        + [pl.BlockSpec(memory_space=pltpu.VMEM)] * len(flat),
        out_specs=pl.BlockSpec(memory_space=pltpu.VMEM),
        scratch_shapes=[pltpu.VMEM((strip_count, 2, rows, columns), BF)],
        compiler_params=params(),
        cost_estimate=cost(10**6, 4 * 10**6),
        name="pack",
    )(slot_strip, *flat)


def insertion_kernel(which, filled, rows_ref, ins_ref, out_ref):
    t = pl.program_id(0)
    columns = rows_ref.shape[-1]
    groups = rows_ref.shape[0] // 2
    width = ins_ref.shape[-1]

    @pl.when(filled[t] == 0)
    def _():
        out_ref[...] = jnp.zeros_like(out_ref)

    @pl.when(filled[t] != 0)
    def _():
        total = None
        for core in range(2):
            lhs = jnp.concatenate(
                [rows_ref[2 * g + core, 0, p] for p in range(2) for g in range(groups)],
                axis=0,
            )
            rhs = ins_ref[0, :, core].reshape(columns, width)
            term = jnp.dot(lhs, rhs, preferred_element_type=F32)
            total = term if total is None else total + term
        out_ref[0] = total.astype(BF).reshape(2, STRIP, width)


def contract(which, filled, received, insertion):
    senders, cap, parts, rows, columns = received.shape
    diagrams, _, width = insertion.shape
    n_mode = 8
    modes = columns // n_mode
    split = insertion.reshape(diagrams, n_mode, 2, modes, width)
    return pl.pallas_call(
        insertion_kernel,
        out_shape=jax.ShapeDtypeStruct((cap, parts, STRIP, width), BF),
        grid_spec=pltpu.PrefetchScalarGridSpec(
            num_scalar_prefetch=2,
            grid=(cap,),
            in_specs=[
                pl.BlockSpec(
                    (senders, 1, parts, rows, columns), lambda t, w, f: (0, t, 0, 0, 0)
                ),
                pl.BlockSpec(
                    (1, n_mode, 2, modes, width), lambda t, w, f: (w[t], 0, 0, 0, 0)
                ),
            ],
            out_specs=pl.BlockSpec(
                (1, parts, STRIP, width), lambda t, w, f: (t, 0, 0, 0)
            ),
        ),
        compiler_params=params(),
        cost_estimate=cost(16 * 10**8, 10**7),
        name="contract",
    )(which, filled, received, split)


def swap(x, axis, bits):
    n = lax.axis_size(axis)
    return lax.ppermute(x, axis, [(i, i ^ bits) for i in range(n)])


def swap_both(x):
    n_mode, n_space = lax.axis_size("mode"), lax.axis_size("space")
    bits = YHI * n_space + CORE
    pairs = [(i, i ^ bits) for i in range(n_mode * n_space)]
    return lax.ppermute(x, ("mode", "space"), pairs)


CHUNKS = ((0, 1), (2, 3))
WAIT = (None, 1)

Z1, Z3, Y1, CORE = 4, 12, 2, 1
X1, X3, YHI = 1, 3, 4


def slots(owner_list, n_space, me_space):
    strip_count = owner_list.shape[0]
    same = owner_list[:, None] == owner_list[None, :]
    order = jnp.arange(strip_count, dtype=jnp.int32)
    earlier = order[None, :] < order[:, None]
    rank = jnp.sum((same & earlier).astype(jnp.int32), axis=1)
    slot = owner_list * CAP + rank
    numbers = jnp.arange(n_space * CAP, dtype=jnp.int32)
    match = slot[None, :] == numbers[:, None]
    slot_strip = jnp.sum(jnp.where(match, order[None, :], 0), axis=1)
    mine = me_space * CAP + jnp.arange(CAP, dtype=jnp.int32)
    my_match = slot[None, :] == mine[:, None]
    my_strip = jnp.sum(jnp.where(my_match, order[None, :], 0), axis=1)
    filled = jnp.sum(my_match.astype(jnp.int32), axis=1)
    return slot_strip, my_strip, filled


def gather(a0, b0):
    a1 = swap(a0, "mode", X1)
    b1 = swap(b0, "mode", X3)
    a2 = swap(jnp.concatenate([a0, a1]), "mode", X3)
    b2 = swap(jnp.concatenate([b0, b1]), "mode", X1)
    return (a0, a1, a2), (b0, b1, b2)


def sum_z(a_keep, a_send, b_keep, b_send):
    a_in = swap(a_send, "space", Z1)
    b_in = swap(b_send, "space", Z3)
    a_pass = (a_keep[1].astype(F32) + a_in[1].astype(F32)).astype(BF)
    b_pass = (b_keep[1].astype(F32) + b_in[1].astype(F32)).astype(BF)
    a_last = swap(a_pass, "space", Z3)
    b_last = swap(b_pass, "space", Z1)
    a_sum = a_keep[0].astype(F32) + a_in[0].astype(F32) + a_last.astype(F32)
    b_sum = b_keep[0].astype(F32) + b_in[0].astype(F32) + b_last.astype(F32)
    return a_sum, b_sum, (a_in, b_in)


def on_device(resident, source, insertion, owners, diag_time, diag_mom):
    slab = resident.shape[3]
    n_space = lax.axis_size("space")
    diagrams = insertion.shape[0]
    blocks = resident.shape[1] // STRIP
    groups = n_space // 2
    me_space = lax.axis_index("space")
    me_mode = lax.axis_index("mode")
    place = [me_space // 4, me_space % 2, me_mode, me_space // 2 % 2]
    meta = jnp.concatenate([diag_time, jnp.stack(place).astype(jnp.int32)])
    cosine, sine = phase_pair(diag_mom, me_space * slab, slab)

    def first_phase(ds, after):
        keep, send = source_slices(ds, meta, cosine, sine, source, after)
        arrived = swap(send, "space", CORE)
        far_keep = swap(keep, "mode", YHI)
        far_arrived = swap_both(send)
        return (keep, far_keep), (arrived, far_arrived)

    def part(pair, lo, hi):
        return jnp.stack([x[lo:hi] for x in pair])

    slot_strip, my_strip, filled = slots(owners[:, 0], n_space, me_space)
    pairs = first_phase(tuple(range(diagrams)), meta)
    beside = swap(resident, "space", CORE)
    vectors = resident_slices(CHUNKS, meta, resident, pairs[0][0], groups)
    across = resident_slices(CHUNKS, meta, beside, pairs[0][0], groups)

    finished, fields, landed = [], (meta, meta), [(meta, meta)]
    for chunk, (ds, own, par) in enumerate(zip(CHUNKS, vectors, across)):
        sides = gather(*(part(pair, ds[0], ds[-1] + 1) for pair in pairs))
        after = fields[:2] if WAIT[chunk] is None else landed[WAIT[chunk]]
        fields = partial_field(len(ds), 0, meta, own, par, *sides, *after)
        a_sum, b_sum, first = sum_z(*fields)
        landed.append(first)
        over_y = swap(jnp.stack([a_sum[:, 1], b_sum[:, 1]]).astype(BF), "space", Y1)
        finished.append((a_sum[:, 0], b_sum[:, 0], over_y))

    outgoing = pack(slot_strip, finished, diagrams * blocks, STRIP // groups)
    outgoing = outgoing.reshape(n_space, CAP, *outgoing.shape[1:])
    received = lax.all_to_all(outgoing, "space", 0, 0, tiled=True)
    return contract(my_strip // blocks, filled, received, insertion)


def solution(mesh):
    in_specs = (
        P(None, "mode", None, "space"),
        P(None, "mode", None, "space"),
        P(),
        P("mode", None),
        P(),
        P(),
    )
    out_specs = P("space", None, "mode", None)
    return jax.shard_map(
        on_device, mesh=mesh, in_specs=in_specs, out_specs=out_specs, check_vma=False
    )
```

```python
import functools
import math

import jax
import jax.numpy as jnp
from jax import lax
from jax.experimental import pallas as pl
from jax.experimental.pallas import tpu as pltpu
from jax.sharding import PartitionSpec as P

STRIP = 128
LX = 96
CAP = 4
BF = jnp.bfloat16
F32 = jnp.float32
VMEM_LIMIT = 48 * 1024 * 1024


def phase_pair(diag_mom, start, count):
    lattice_positions = (start + jnp.arange(count, dtype=jnp.int32)) % LX
    turns = diag_mom[:, None] * lattice_positions[None, :] % LX
    angle = 2.0 * math.pi / LX * turns.astype(F32)
    return jnp.cos(angle), jnp.sin(angle)


def params():
    return pltpu.CompilerParams(vmem_limit_bytes=VMEM_LIMIT)


def cost(flops, size):
    return pl.CostEstimate(flops=flops, bytes_accessed=size, transcendentals=0)


LANES = 128


def widen(ref, wide):
    parts, rows, times, _ = ref.shape
    for p in range(parts):
        for h in range(wide.shape[1]):
            x = ref[p, :, :, h * LANES : (h + 1) * LANES]
            wide[p, h] = x.astype(F32).reshape(rows * times, LANES)


def narrow(wide, p, rows):
    return jnp.concatenate([wide[p, h, rows, :] for h in range(wide.shape[1])], axis=1)


def source_kernel(ds, meta, cos_ref, sin_ref, src_ref, after_ref, keep_ref, send_ref, wide):
    _, modes, times, sites = src_ref.shape
    half = modes // 2
    widen(src_ref, wide)
    core = meta[5]
    for n, d in enumerate(ds):
        c = cos_ref[d : d + 1, :]
        s = sin_ref[d : d + 1, :]
        for ref, who in ((keep_ref, core), (send_ref, 1 - core)):
            rows = pl.ds(who * (half * times) + meta[d], half, stride=times)
            re = narrow(wide, 0, rows)
            im = narrow(wide, 1, rows)
            ref[n, :, 0:sites] = (re * c + im * s).astype(BF)
            ref[n, :, sites : 2 * sites] = (im * c - re * s).astype(BF)


def source_slices(ds, meta, cosine, sine, source, after):
    parts, modes, times, sites = source.shape
    piece = jax.ShapeDtypeStruct((len(ds), modes // 2, parts * sites), BF)
    return pl.pallas_call(
        functools.partial(source_kernel, ds),
        out_shape=(piece, piece),
        in_specs=[pl.BlockSpec(memory_space=pltpu.SMEM)]
        + [pl.BlockSpec(memory_space=pltpu.VMEM)] * 3
        + [pl.BlockSpec(memory_space=pl.ANY)],
        out_specs=[pl.BlockSpec(memory_space=pltpu.VMEM)] * 2,
        scratch_shapes=[pltpu.VMEM((parts, sites // LANES, modes * times, LANES), F32)],
        compiler_params=params(),
        cost_estimate=cost(10**6, 2 * 10**6),
        name="source_slices",
    )(meta, cosine, sine, source, after)


def resident_kernel(chunks, meta, res_ref, after_ref, *refs):
    outs, wide = refs[:-1], refs[-1]
    parts, strip, times, sites = res_ref.shape
    rows = outs[0].shape[3]
    groups = strip // rows
    z, y = meta[4], meta[7]
    widen(res_ref, wide)
    for out_ref, n, d in [(r, n, d) for r, ds in zip(outs, chunks) for n, d in enumerate(ds)]:
        for p in range(parts):
            x = narrow(wide, p, pl.ds(meta[d], strip, stride=times)).astype(BF)
            for g in range(groups):
                at = ((g % 2) ^ y) * (groups // 2) + ((g // 2) ^ z)
                out_ref[n, at, 0, :, p * sites : (p + 1) * sites] = x[
                    g * rows : (g + 1) * rows
                ]


def resident_slices(chunks, meta, resident, after, groups):
    parts, res_dev, times, sites = resident.shape
    blocks = res_dev // STRIP
    rows = STRIP // groups
    shapes = [(len(ds), groups, blocks, rows, parts * sites) for ds in chunks]
    return pl.pallas_call(
        functools.partial(resident_kernel, chunks),
        out_shape=[jax.ShapeDtypeStruct(shape, BF) for shape in shapes],
        grid_spec=pltpu.PrefetchScalarGridSpec(
            num_scalar_prefetch=1,
            grid=(blocks,),
            in_specs=[
                pl.BlockSpec((parts, STRIP, times, sites), lambda b, meta: (0, b, 0, 0)),
                pl.BlockSpec(memory_space=pl.ANY),
            ],
            out_specs=[
                pl.BlockSpec((*shape[:2], 1, *shape[3:]), lambda b, meta: (0, 0, b, 0, 0))
                for shape in shapes
            ],
            scratch_shapes=[pltpu.VMEM((parts, sites // LANES, STRIP * times, LANES), F32)],
        ),
        compiler_params=params(),
        cost_estimate=cost(30 * 10**9, 13 * 10**6),
        name="resident_slices",
    )(meta, resident, after)


PLACES = (
    ((0, 4), (1, 5), (3, 7, 2, 6)),
    ((0, 4), (3, 7), (1, 5, 2, 6)),
)


def field_kernel(meta, own_ref, par_ref, a0, a1, a2, b0, b1, b2, after_a, after_b,
                 a_keep, a_send, b_keep, b_send, real_rhs, imag_rhs):
    me = meta[6]
    _, groups, blocks, rows, width = own_ref.shape
    sites = width // 2
    columns = real_rhs.shape[1] * real_rhs.shape[2]
    for side, arrays in enumerate(((a0, a1, a2), (b0, b1, b2))):
        for ref, places in zip(arrays, PLACES[side]):
            for n, place in enumerate(places):
                at = me ^ place
                v = ref[n, 0]
                real_rhs[side, at] = v
                imag_rhs[side, at, :, 0:sites] = v[:, sites:]
                imag_rhs[side, at, :, sites:] = -v[:, 0:sites]

    zs = groups // 2
    tall = blocks * rows
    for k in range(2):
        left = [x[0, k * zs : (k + 1) * zs].reshape(zs * tall, width) for x in (own_ref, par_ref)]

        def product(rhs, left=left):
            total = None
            for n, x in enumerate(left):
                term = lax.dot_general(
                    x,
                    rhs[n].reshape(columns, width),
                    (((1,), (1,)), ((), ())),
                    preferred_element_type=F32,
                )
                total = term if total is None else total + term
            return total.astype(BF).reshape(zs, tall, columns)

        real = product(real_rhs)
        imag = product(imag_rhs)
        a_keep[0, 0, k] = real[0]
        a_send[0, 0, k] = real[1]
        a_send[1, 0, k] = real[2]
        a_keep[1, 0, k] = real[3]
        b_keep[0, 0, k] = imag[0]
        b_keep[1, 0, k] = imag[1]
        b_send[1, 0, k] = imag[2]
        b_send[0, 0, k] = imag[3]


def partial_field(n, at, meta, own, par, side_a, side_b, after_a, after_b):
    _, groups, blocks, rows, width = own.shape
    modes = side_a[0].shape[2]
    columns = 8 * modes
    out = jax.ShapeDtypeStruct((2, n, 2, blocks * rows, columns), BF)
    left = pl.BlockSpec(
        (1, groups, blocks, rows, width), lambda i, meta: (at + i, 0, 0, 0, 0)
    )

    def piece(x):
        return pl.BlockSpec((x.shape[0], 1, modes, width), lambda i, meta: (0, i, 0, 0))

    return pl.pallas_call(
        field_kernel,
        out_shape=(out,) * 4,
        grid_spec=pltpu.PrefetchScalarGridSpec(
            num_scalar_prefetch=1,
            grid=(n,),
            in_specs=[left, left]
            + [piece(x) for x in (*side_a, *side_b)]
            + [pl.BlockSpec(memory_space=pl.ANY)] * 2,
            out_specs=[
                pl.BlockSpec((2, 1, *out.shape[2:]), lambda i, meta: (0, i, 0, 0, 0))
            ]
            * 4,
            scratch_shapes=[pltpu.VMEM((2, 8, modes, width), BF)] * 2,
        ),
        compiler_params=params(),
        cost_estimate=cost(n * 2 * 1024 * 1024 * 768, n * 5 * 10**6),
        name="field",
    )(meta, own, par, *side_a, *side_b, after_a, after_b)


def pack_kernel(counts, slot_ref, *refs):
    ins, out_ref, strips = list(refs[:-2]), refs[-2], refs[-1]
    rows, columns = strips.shape[2:]
    at = 0
    for n, size in counts:
        sums = [ins.pop(0) for _ in range(2)]
        other = ins.pop(0) if size == 3 else None
        blocks = sums[0].shape[1] // rows
        for d in range(n):
            for p in range(2):
                total = sums[p][d]
                if other is not None:
                    total = total + other[p, d].astype(F32)
                strips[at : at + blocks, p] = total.astype(BF).reshape(
                    blocks, rows, columns
                )
            at += blocks

    def one(slot, carry):
        out_ref[slot] = strips[slot_ref[slot]]
        return carry

    lax.fori_loop(0, out_ref.shape[0], one, 0)


def pack(slot_strip, finished, strip_count, rows):
    columns = finished[0][0].shape[-1]
    flat = [x for group in finished for x in group]
    counts = [(group[0].shape[0], len(group)) for group in finished]
    return pl.pallas_call(
        functools.partial(pack_kernel, counts),
        out_shape=jax.ShapeDtypeStruct((slot_strip.shape[0], 2, rows, columns), BF),
        in_specs=[pl.BlockSpec(memory_space=pltpu.SMEM)]
        + [pl.BlockSpec(memory_space=pltpu.VMEM)] * len(flat),
        out_specs=pl.BlockSpec(memory_space=pltpu.VMEM),
        scratch_shapes=[pltpu.VMEM((strip_count, 2, rows, columns), BF)],
        compiler_params=params(),
        cost_estimate=cost(10**6, 4 * 10**6),
        name="pack",
    )(slot_strip, *flat)


def insertion_kernel(which, filled, rows_ref, ins_ref, out_ref):
    t = pl.program_id(0)
    columns = rows_ref.shape[-1]
    groups = rows_ref.shape[0] // 2
    width = ins_ref.shape[-1]

    @pl.when(filled[t] == 0)
    def _():
        out_ref[...] = jnp.zeros_like(out_ref)

    @pl.when(filled[t] != 0)
    def _():
        total = None
        for core in range(2):
            lhs = jnp.concatenate(
                [rows_ref[2 * g + core, 0, p] for p in range(2) for g in range(groups)],
                axis=0,
            )
            rhs = ins_ref[0, :, core].reshape(columns, width)
            term = jnp.dot(lhs, rhs, preferred_element_type=F32)
            total = term if total is None else total + term
        out_ref[0] = total.astype(BF).reshape(2, STRIP, width)


def contract(which, filled, received, insertion):
    senders, cap, parts, rows, columns = received.shape
    diagrams, _, width = insertion.shape
    n_mode = 8
    modes = columns // n_mode
    split = insertion.reshape(diagrams, n_mode, 2, modes, width)
    return pl.pallas_call(
        insertion_kernel,
        out_shape=jax.ShapeDtypeStruct((cap, parts, STRIP, width), BF),
        grid_spec=pltpu.PrefetchScalarGridSpec(
            num_scalar_prefetch=2,
            grid=(cap,),
            in_specs=[
                pl.BlockSpec(
                    (senders, 1, parts, rows, columns), lambda t, w, f: (0, t, 0, 0, 0)
                ),
                pl.BlockSpec(
                    (1, n_mode, 2, modes, width), lambda t, w, f: (w[t], 0, 0, 0, 0)
                ),
            ],
            out_specs=pl.BlockSpec(
                (1, parts, STRIP, width), lambda t, w, f: (t, 0, 0, 0)
            ),
        ),
        compiler_params=params(),
        cost_estimate=cost(16 * 10**8, 10**7),
        name="contract",
    )(which, filled, received, split)


def swap(x, axis, bits):
    n = lax.axis_size(axis)
    return lax.ppermute(x, axis, [(i, i ^ bits) for i in range(n)])


def swap_both(x):
    n_mode, n_space = lax.axis_size("mode"), lax.axis_size("space")
    bits = YHI * n_space + CORE
    pairs = [(i, i ^ bits) for i in range(n_mode * n_space)]
    return lax.ppermute(x, ("mode", "space"), pairs)


CHUNKS = ((0, 1), (2, 3))
WAIT = (None, 1)

Z1, Z3, Y1, CORE = 4, 12, 2, 1
X1, X3, YHI = 1, 3, 4


def slots(owner_list, n_space, me_space):
    strip_count = owner_list.shape[0]
    same = owner_list[:, None] == owner_list[None, :]
    order = jnp.arange(strip_count, dtype=jnp.int32)
    earlier = order[None, :] < order[:, None]
    rank = jnp.sum((same & earlier).astype(jnp.int32), axis=1)
    slot = owner_list * CAP + rank
    numbers = jnp.arange(n_space * CAP, dtype=jnp.int32)
    match = slot[None, :] == numbers[:, None]
    slot_strip = jnp.sum(jnp.where(match, order[None, :], 0), axis=1)
    mine = me_space * CAP + jnp.arange(CAP, dtype=jnp.int32)
    my_match = slot[None, :] == mine[:, None]
    my_strip = jnp.sum(jnp.where(my_match, order[None, :], 0), axis=1)
    filled = jnp.sum(my_match.astype(jnp.int32), axis=1)
    return slot_strip, my_strip, filled


def gather(a0, b0):
    a1 = swap(a0, "mode", X1)
    b1 = swap(b0, "mode", X3)
    a2 = swap(jnp.concatenate([a0, a1]), "mode", X3)
    b2 = swap(jnp.concatenate([b0, b1]), "mode", X1)
    return (a0, a1, a2), (b0, b1, b2)


def sum_z(a_keep, a_send, b_keep, b_send):
    a_in = swap(a_send, "space", Z1)
    b_in = swap(b_send, "space", Z3)
    a_pass = (a_keep[1].astype(F32) + a_in[1].astype(F32)).astype(BF)
    b_pass = (b_keep[1].astype(F32) + b_in[1].astype(F32)).astype(BF)
    a_last = swap(a_pass, "space", Z3)
    b_last = swap(b_pass, "space", Z1)
    a_sum = a_keep[0].astype(F32) + a_in[0].astype(F32) + a_last.astype(F32)
    b_sum = b_keep[0].astype(F32) + b_in[0].astype(F32) + b_last.astype(F32)
    return a_sum, b_sum, (b_in, b_in)


def on_device(resident, source, insertion, owners, diag_time, diag_mom):
    slab = resident.shape[3]
    n_space = lax.axis_size("space")
    diagrams = insertion.shape[0]
    blocks = resident.shape[1] // STRIP
    groups = n_space // 2
    me_space = lax.axis_index("space")
    me_mode = lax.axis_index("mode")
    place = [me_space // 4, me_space % 2, me_mode, me_space // 2 % 2]
    meta = jnp.concatenate([diag_time, jnp.stack(place).astype(jnp.int32)])
    cosine, sine = phase_pair(diag_mom, me_space * slab, slab)

    def first_phase(ds, after):
        keep, send = source_slices(ds, meta, cosine, sine, source, after)
        arrived = swap(send, "space", CORE)
        far_keep = swap(keep, "mode", YHI)
        far_arrived = swap_both(send)
        return (keep, far_keep), (arrived, far_arrived)

    def part(pair, lo, hi):
        return jnp.stack([x[lo:hi] for x in pair])

    slot_strip, my_strip, filled = slots(owners[:, 0], n_space, me_space)
    pairs = first_phase(tuple(range(diagrams)), meta)
    beside = swap(resident, "space", CORE)
    vectors = resident_slices(CHUNKS, meta, resident, pairs[0][0], groups)
    across = resident_slices(CHUNKS, meta, beside, pairs[0][0], groups)

    finished, fields, landed = [], (meta, meta), [(meta, meta)]
    for chunk, (ds, own, par) in enumerate(zip(CHUNKS, vectors, across)):
        sides = gather(*(part(pair, ds[0], ds[-1] + 1) for pair in pairs))
        after = fields[:2] if WAIT[chunk] is None else landed[WAIT[chunk]]
        fields = partial_field(len(ds), 0, meta, own, par, *sides, *after)
        a_sum, b_sum, first = sum_z(*fields)
        landed.append(first)
        over_y = swap(jnp.stack([a_sum[:, 1], b_sum[:, 1]]).astype(BF), "space", Y1)
        finished.append((a_sum[:, 0], b_sum[:, 0], over_y))

    outgoing = pack(slot_strip, finished, diagrams * blocks, STRIP // groups)
    outgoing = outgoing.reshape(n_space, CAP, *outgoing.shape[1:])
    received = lax.all_to_all(outgoing, "space", 0, 0, tiled=True)
    return contract(my_strip // blocks, filled, received, insertion)


def solution(mesh):
    in_specs = (
        P(None, "mode", None, "space"),
        P(None, "mode", None, "space"),
        P(),
        P("mode", None),
        P(),
        P(),
    )
    out_specs = P("space", None, "mode", None)
    return jax.shard_map(
        on_device, mesh=mesh, in_specs=in_specs, out_specs=out_specs, check_vma=False
    )
```

```python
import functools
import math

import jax
import jax.numpy as jnp
from jax import lax
from jax.experimental import pallas as pl
from jax.experimental.pallas import tpu as pltpu
from jax.sharding import PartitionSpec as P

STRIP = 128
LX = 96
CAP = 4
BF = jnp.bfloat16
F32 = jnp.float32
VMEM_LIMIT = 48 * 1024 * 1024


def phase_pair(diag_mom, start, count):
    lattice_positions = (start + jnp.arange(count, dtype=jnp.int32)) % LX
    turns = diag_mom[:, None] * lattice_positions[None, :] % LX
    angle = 2.0 * math.pi / LX * turns.astype(F32)
    return jnp.cos(angle), jnp.sin(angle)


def params():
    return pltpu.CompilerParams(vmem_limit_bytes=VMEM_LIMIT)


def cost(flops, size):
    return pl.CostEstimate(flops=flops, bytes_accessed=size, transcendentals=0)


LANES = 128


def widen(ref, wide):
    parts, rows, times, _ = ref.shape
    for p in range(parts):
        for h in range(wide.shape[1]):
            x = ref[p, :, :, h * LANES : (h + 1) * LANES]
            wide[p, h] = x.astype(F32).reshape(rows * times, LANES)


def narrow(wide, p, rows):
    return jnp.concatenate([wide[p, h, rows, :] for h in range(wide.shape[1])], axis=1)


def source_kernel(ds, meta, cos_ref, sin_ref, src_ref, after_ref, keep_ref, send_ref, wide):
    _, modes, times, sites = src_ref.shape
    half = modes // 2
    widen(src_ref, wide)
    core = meta[5]
    for n, d in enumerate(ds):
        c = cos_ref[d : d + 1, :]
        s = sin_ref[d : d + 1, :]
        for ref, who in ((keep_ref, core), (send_ref, 1 - core)):
            rows = pl.ds(who * (half * times) + meta[d], half, stride=times)
            re = narrow(wide, 0, rows)
            im = narrow(wide, 1, rows)
            ref[n, :, 0:sites] = (re * c + im * s).astype(BF)
            ref[n, :, sites : 2 * sites] = (im * c - re * s).astype(BF)


def source_slices(ds, meta, cosine, sine, source, after):
    parts, modes, times, sites = source.shape
    piece = jax.ShapeDtypeStruct((len(ds), modes // 2, parts * sites), BF)
    return pl.pallas_call(
        functools.partial(source_kernel, ds),
        out_shape=(piece, piece),
        in_specs=[pl.BlockSpec(memory_space=pltpu.SMEM)]
        + [pl.BlockSpec(memory_space=pltpu.VMEM)] * 3
        + [pl.BlockSpec(memory_space=pl.ANY)],
        out_specs=[pl.BlockSpec(memory_space=pltpu.VMEM)] * 2,
        scratch_shapes=[pltpu.VMEM((parts, sites // LANES, modes * times, LANES), F32)],
        compiler_params=params(),
        cost_estimate=cost(10**6, 2 * 10**6),
        name="source_slices",
    )(meta, cosine, sine, source, after)


def resident_kernel(chunks, meta, res_ref, after_ref, *refs):
    outs, wide = refs[:-1], refs[-1]
    parts, strip, times, sites = res_ref.shape
    rows = outs[0].shape[3]
    groups = strip // rows
    z, y = meta[4], meta[7]
    widen(res_ref, wide)
    for out_ref, n, d in [(r, n, d) for r, ds in zip(outs, chunks) for n, d in enumerate(ds)]:
        for p in range(parts):
            x = narrow(wide, p, pl.ds(meta[d], strip, stride=times)).astype(BF)
            for g in range(groups):
                at = ((g % 2) ^ y) * (groups // 2) + ((g // 2) ^ z)
                out_ref[n, at, 0, :, p * sites : (p + 1) * sites] = x[
                    g * rows : (g + 1) * rows
                ]


def resident_slices(chunks, meta, resident, after, groups):
    parts, res_dev, times, sites = resident.shape
    blocks = res_dev // STRIP
    rows = STRIP // groups
    shapes = [(len(ds), groups, blocks, rows, parts * sites) for ds in chunks]
    return pl.pallas_call(
        functools.partial(resident_kernel, chunks),
        out_shape=[jax.ShapeDtypeStruct(shape, BF) for shape in shapes],
        grid_spec=pltpu.PrefetchScalarGridSpec(
            num_scalar_prefetch=1,
            grid=(blocks,),
            in_specs=[
                pl.BlockSpec((parts, STRIP, times, sites), lambda b, meta: (0, b, 0, 0)),
                pl.BlockSpec(memory_space=pl.ANY),
            ],
            out_specs=[
                pl.BlockSpec((*shape[:2], 1, *shape[3:]), lambda b, meta: (0, 0, b, 0, 0))
                for shape in shapes
            ],
            scratch_shapes=[pltpu.VMEM((parts, sites // LANES, STRIP * times, LANES), F32)],
        ),
        compiler_params=params(),
        cost_estimate=cost(30 * 10**9, 13 * 10**6),
        name="resident_slices",
    )(meta, resident, after)


PLACES = (
    ((0, 4), (1, 5), (3, 7, 2, 6)),
    ((0, 4), (3, 7), (1, 5, 2, 6)),
)


def field_kernel(meta, own_ref, par_ref, a0, a1, a2, b0, b1, b2, after_a, after_b,
                 a_keep, a_send, b_keep, b_send, real_rhs, imag_rhs):
    me = meta[6]
    _, groups, blocks, rows, width = own_ref.shape
    sites = width // 2
    columns = real_rhs.shape[1] * real_rhs.shape[2]
    @pl.when(pl.program_id(1) == 0)
    def _():
        for side, arrays in enumerate(((a0, a1, a2), (b0, b1, b2))):
            for ref, places in zip(arrays, PLACES[side]):
                for n, place in enumerate(places):
                    at = me ^ place
                    v = ref[n, 0]
                    real_rhs[side, at] = v
                    imag_rhs[side, at, :, 0:sites] = v[:, sites:]
                    imag_rhs[side, at, :, sites:] = -v[:, 0:sites]

    zs = groups
    tall = blocks * rows
    left = [x[0].reshape(zs * tall, width) for x in (own_ref, par_ref)]

    def product(rhs, left=left):
        total = None
        for n, x in enumerate(left):
            term = lax.dot_general(
                x,
                rhs[n].reshape(columns, width),
                (((1,), (1,)), ((), ())),
                preferred_element_type=F32,
            )
            total = term if total is None else total + term
        return total.astype(BF).reshape(zs, tall, columns)

    real = product(real_rhs)
    imag = product(imag_rhs)
    a_keep[0, 0, 0] = real[0]
    a_send[0, 0, 0] = real[1]
    a_send[1, 0, 0] = real[2]
    a_keep[1, 0, 0] = real[3]
    b_keep[0, 0, 0] = imag[0]
    b_keep[1, 0, 0] = imag[1]
    b_send[1, 0, 0] = imag[2]
    b_send[0, 0, 0] = imag[3]


def partial_field(n, at, meta, own, par, side_a, side_b, after_a, after_b):
    _, groups, blocks, rows, width = own.shape
    modes = side_a[0].shape[2]
    columns = 8 * modes
    out = jax.ShapeDtypeStruct((2, n, 2, blocks * rows, columns), BF)
    left = pl.BlockSpec(
        (1, groups // 2, blocks, rows, width), lambda i, k, meta: (at + i, k, 0, 0, 0)
    )

    def piece(x):
        return pl.BlockSpec((x.shape[0], 1, modes, width), lambda i, k, meta: (0, i, 0, 0))

    return pl.pallas_call(
        field_kernel,
        out_shape=(out,) * 4,
        grid_spec=pltpu.PrefetchScalarGridSpec(
            num_scalar_prefetch=1,
            grid=(n, 2),
            in_specs=[left, left]
            + [piece(x) for x in (*side_a, *side_b)]
            + [pl.BlockSpec(memory_space=pl.ANY)] * 2,
            out_specs=[
                pl.BlockSpec((2, 1, 1, *out.shape[3:]), lambda i, k, meta: (0, i, k, 0, 0))
            ]
            * 4,
            scratch_shapes=[pltpu.VMEM((2, 8, modes, width), BF)] * 2,
        ),
        compiler_params=params(),
        cost_estimate=cost(n * 2 * 1024 * 1024 * 768, n * 5 * 10**6),
        name="field",
    )(meta, own, par, *side_a, *side_b, after_a, after_b)


def pack_kernel(counts, slot_ref, *refs):
    ins, out_ref, strips = list(refs[:-2]), refs[-2], refs[-1]
    rows, columns = strips.shape[2:]
    at = 0
    for n, size in counts:
        sums = [ins.pop(0) for _ in range(2)]
        other = ins.pop(0) if size == 3 else None
        blocks = sums[0].shape[1] // rows
        for d in range(n):
            for p in range(2):
                total = sums[p][d]
                if other is not None:
                    total = total + other[p, d].astype(F32)
                strips[at : at + blocks, p] = total.astype(BF).reshape(
                    blocks, rows, columns
                )
            at += blocks

    def one(slot, carry):
        out_ref[slot] = strips[slot_ref[slot]]
        return carry

    lax.fori_loop(0, out_ref.shape[0], one, 0)


def pack(slot_strip, finished, strip_count, rows):
    columns = finished[0][0].shape[-1]
    flat = [x for group in finished for x in group]
    counts = [(group[0].shape[0], len(group)) for group in finished]
    return pl.pallas_call(
        functools.partial(pack_kernel, counts),
        out_shape=jax.ShapeDtypeStruct((slot_strip.shape[0], 2, rows, columns), BF),
        in_specs=[pl.BlockSpec(memory_space=pltpu.SMEM)]
        + [pl.BlockSpec(memory_space=pltpu.VMEM)] * len(flat),
        out_specs=pl.BlockSpec(memory_space=pltpu.VMEM),
        scratch_shapes=[pltpu.VMEM((strip_count, 2, rows, columns), BF)],
        compiler_params=params(),
        cost_estimate=cost(10**6, 4 * 10**6),
        name="pack",
    )(slot_strip, *flat)


def insertion_kernel(which, filled, rows_ref, ins_ref, out_ref):
    t = pl.program_id(0)
    columns = rows_ref.shape[-1]
    groups = rows_ref.shape[0] // 2
    width = ins_ref.shape[-1]

    @pl.when(filled[t] == 0)
    def _():
        out_ref[...] = jnp.zeros_like(out_ref)

    @pl.when(filled[t] != 0)
    def _():
        total = None
        for core in range(2):
            lhs = jnp.concatenate(
                [rows_ref[2 * g + core, 0, p] for p in range(2) for g in range(groups)],
                axis=0,
            )
            rhs = ins_ref[0, :, core].reshape(columns, width)
            term = jnp.dot(lhs, rhs, preferred_element_type=F32)
            total = term if total is None else total + term
        out_ref[0] = total.astype(BF).reshape(2, STRIP, width)


def contract(which, filled, received, insertion):
    senders, cap, parts, rows, columns = received.shape
    diagrams, _, width = insertion.shape
    n_mode = 8
    modes = columns // n_mode
    split = insertion.reshape(diagrams, n_mode, 2, modes, width)
    return pl.pallas_call(
        insertion_kernel,
        out_shape=jax.ShapeDtypeStruct((cap, parts, STRIP, width), BF),
        grid_spec=pltpu.PrefetchScalarGridSpec(
            num_scalar_prefetch=2,
            grid=(cap,),
            in_specs=[
                pl.BlockSpec(
                    (senders, 1, parts, rows, columns), lambda t, w, f: (0, t, 0, 0, 0)
                ),
                pl.BlockSpec(
                    (1, n_mode, 2, modes, width), lambda t, w, f: (w[t], 0, 0, 0, 0)
                ),
            ],
            out_specs=pl.BlockSpec(
                (1, parts, STRIP, width), lambda t, w, f: (t, 0, 0, 0)
            ),
        ),
        compiler_params=params(),
        cost_estimate=cost(16 * 10**8, 10**7),
        name="contract",
    )(which, filled, received, split)


def swap(x, axis, bits):
    n = lax.axis_size(axis)
    return lax.ppermute(x, axis, [(i, i ^ bits) for i in range(n)])


def swap_both(x):
    n_mode, n_space = lax.axis_size("mode"), lax.axis_size("space")
    bits = YHI * n_space + CORE
    pairs = [(i, i ^ bits) for i in range(n_mode * n_space)]
    return lax.ppermute(x, ("mode", "space"), pairs)


CHUNKS = ((0, 1), (2, 3))
WAIT = (None, 1)

Z1, Z3, Y1, CORE = 4, 12, 2, 1
X1, X3, YHI = 1, 3, 4


def slots(owner_list, n_space, me_space):
    strip_count = owner_list.shape[0]
    same = owner_list[:, None] == owner_list[None, :]
    order = jnp.arange(strip_count, dtype=jnp.int32)
    earlier = order[None, :] < order[:, None]
    rank = jnp.sum((same & earlier).astype(jnp.int32), axis=1)
    slot = owner_list * CAP + rank
    numbers = jnp.arange(n_space * CAP, dtype=jnp.int32)
    match = slot[None, :] == numbers[:, None]
    slot_strip = jnp.sum(jnp.where(match, order[None, :], 0), axis=1)
    mine = me_space * CAP + jnp.arange(CAP, dtype=jnp.int32)
    my_match = slot[None, :] == mine[:, None]
    my_strip = jnp.sum(jnp.where(my_match, order[None, :], 0), axis=1)
    filled = jnp.sum(my_match.astype(jnp.int32), axis=1)
    return slot_strip, my_strip, filled


def gather(a0, b0):
    a1 = swap(a0, "mode", X1)
    b1 = swap(b0, "mode", X3)
    a2 = swap(jnp.concatenate([a0, a1]), "mode", X3)
    b2 = swap(jnp.concatenate([b0, b1]), "mode", X1)
    return (a0, a1, a2), (b0, b1, b2)


def sum_z(a_keep, a_send, b_keep, b_send):
    a_in = swap(a_send, "space", Z1)
    b_in = swap(b_send, "space", Z3)
    a_pass = (a_keep[1].astype(F32) + a_in[1].astype(F32)).astype(BF)
    b_pass = (b_keep[1].astype(F32) + b_in[1].astype(F32)).astype(BF)
    a_last = swap(a_pass, "space", Z3)
    b_last = swap(b_pass, "space", Z1)
    a_sum = a_keep[0].astype(F32) + a_in[0].astype(F32) + a_last.astype(F32)
    b_sum = b_keep[0].astype(F32) + b_in[0].astype(F32) + b_last.astype(F32)
    return a_sum, b_sum, (b_in, b_in)


def on_device(resident, source, insertion, owners, diag_time, diag_mom):
    slab = resident.shape[3]
    n_space = lax.axis_size("space")
    diagrams = insertion.shape[0]
    blocks = resident.shape[1] // STRIP
    groups = n_space // 2
    me_space = lax.axis_index("space")
    me_mode = lax.axis_index("mode")
    place = [me_space // 4, me_space % 2, me_mode, me_space // 2 % 2]
    meta = jnp.concatenate([diag_time, jnp.stack(place).astype(jnp.int32)])
    cosine, sine = phase_pair(diag_mom, me_space * slab, slab)

    def first_phase(ds, after):
        keep, send = source_slices(ds, meta, cosine, sine, source, after)
        arrived = swap(send, "space", CORE)
        far_keep = swap(keep, "mode", YHI)
        far_arrived = swap_both(send)
        return (keep, far_keep), (arrived, far_arrived)

    def part(pair, lo, hi):
        return jnp.stack([x[lo:hi] for x in pair])

    slot_strip, my_strip, filled = slots(owners[:, 0], n_space, me_space)
    pairs = first_phase(tuple(range(diagrams)), meta)
    beside = swap(resident, "space", CORE)
    vectors = resident_slices(CHUNKS, meta, resident, pairs[0][0], groups)
    across = resident_slices(CHUNKS, meta, beside, pairs[0][0], groups)

    finished, fields, landed = [], (meta, meta), [(meta, meta)]
    for chunk, (ds, own, par) in enumerate(zip(CHUNKS, vectors, across)):
        sides = gather(*(part(pair, ds[0], ds[-1] + 1) for pair in pairs))
        after = fields[:2] if WAIT[chunk] is None else landed[WAIT[chunk]]
        fields = partial_field(len(ds), 0, meta, own, par, *sides, *after)
        a_sum, b_sum, first = sum_z(*fields)
        landed.append(first)
        over_y = swap(jnp.stack([a_sum[:, 1], b_sum[:, 1]]).astype(BF), "space", Y1)
        finished.append((a_sum[:, 0], b_sum[:, 0], over_y))

    outgoing = pack(slot_strip, finished, diagrams * blocks, STRIP // groups)
    outgoing = outgoing.reshape(n_space, CAP, *outgoing.shape[1:])
    received = lax.all_to_all(outgoing, "space", 0, 0, tiled=True)
    return contract(my_strip // blocks, filled, received, insertion)


def solution(mesh):
    in_specs = (
        P(None, "mode", None, "space"),
        P(None, "mode", None, "space"),
        P(),
        P("mode", None),
        P(),
        P(),
    )
    out_specs = P("space", None, "mode", None)
    return jax.shard_map(
        on_device, mesh=mesh, in_specs=in_specs, out_specs=out_specs, check_vma=False
    )
```
